128 devices in a mesh: ctx: 32 (over y, x, z_lo), tp: 4 (over z_hi, core).
Axes of the slice: x: 4, y: 4, z: 4 (z_hi: 2, z_lo: 2; z = z_hi * 2 + z_lo), core: 2. Of those that a mesh axis runs over, the one named last changes fastest.
Arguments:
- streams: bfloat16 [3, 4096, 65536], P(None, 'tp', 'ctx'), parts along dimension 1, may hold values from -6 to 6
- short_filters: float32 [3, 3, 4096], P(None, None, 'tp'), parts along dimension 2, may hold values from -3 to 3
- residues: float32 [16, 4096], P(None, 'tp'), parts along dimension 1, may hold values from -1 to 1
- rates: float32 [16, 4096], P(None, 'tp'), parts along dimension 1, may hold values from 3.0517579e-06 to 0.05
- skip: float32 [4096], P('tp'), parts along dimension 0, may hold values from 0.5 to 1.5
Outputs:
- output: bfloat16 [4096, 65536], P('tp', 'ctx'), parts along dimension 0
The draws below stay inside these ranges and needn't reach their ends.
There are 4 independent parts, one for each index of `tp`. The reference program is written for one: setup_inputs(seed, part) draws one part's arguments, and reference() takes and returns one part's arrays. A program takes and returns all parts, laid end to end along the dimension named above; each array names one. Nothing has to cross between parts.
All inputs are finite; a program needn't handle non-finite values.
Results may differ from the reference program's by a relative error of at most 0.0064.
Values may be sent and summed in bfloat16 or wider, within the bound.
No kernel may reach another device: no remote copies, remote signals or barrier semaphores. Data moves between devices by JAX's collectives and lax.ppermute only.
A program may use at most 192 MiB of HBM per device.

```python
import math
import jax
import jax.numpy as jnp
from jax import lax

C = 1024
MODES = 16
SHORT = 3
SEQ = 65536


def level_of(rng, shape, shards, least, largest):
    def one(dim, shards_of):
        heights = jax.random.uniform(jax.random.fold_in(jax.random.fold_in(rng, 6), dim), (shards_of,), jnp.float32, least / len(shards), largest / len(shards))
        return jnp.repeat(jnp.exp(heights), shape[dim] // shards_of).reshape((-1,) + (1,) * (len(shape) - dim - 1))

    level = one(*shards[0])
    for cut in shards[1:]:
        level = level * one(*cut)
    return level


def normal_values(stream_key, shape, width, most, cuts=(), kind=jnp.bfloat16):
    level = level_of(stream_key, shape, cuts, -0.22, 0.18) if cuts else 1.0
    entries = jax.random.normal(stream_key, shape, jnp.float32) * width * level
    return jnp.minimum(jnp.maximum(entries, -most), most).astype(kind)


def setup_inputs(seed: int = 0, part: int = 0) -> dict:
    seeds = jax.random.split(jax.random.key(seed), 6)
    part_keys = jax.random.split(jax.random.fold_in(seeds[5], part), 6)
    streams = normal_values(part_keys[0], (3, C, SEQ), 1.0, 6.0, ((2, 32),))
    short_filters = normal_values(part_keys[1], (3, SHORT, C), 0.6, 3.0, (), jnp.float32)
    residues = normal_values(part_keys[2], (MODES, C), 0.25, 1.0, (), jnp.float32)
    rates = jnp.clip(jnp.exp(jax.random.uniform(part_keys[3], (MODES, C), jnp.float32, math.log(3.051757857974735e-06), math.log(0.05))), 3.051757857974735e-06, 0.05)
    skip = jnp.clip(jax.random.uniform(part_keys[4], (C,), jnp.float32, 0.5, 1.5), 0.5, 1.5)
    return {"streams": streams, "short_filters": short_filters, "residues": residues, "rates": rates, "skip": skip}


def reference(streams, short_filters, residues, rates, skip):
    length = streams.shape[2]
    padded = jnp.pad(streams.astype(jnp.float32), ((0, 0), (0, 0), (SHORT - 1, 0)))
    filtered = jnp.zeros(streams.shape, jnp.float32)
    for offset in range(SHORT):
        begin = SHORT - 1 - offset
        filtered = filtered + short_filters[:, offset, :, None] * padded[:, :, begin:begin + length]
    gated = lax.optimization_barrier((filtered[1] * filtered[2]).astype(jnp.bfloat16))
    query = lax.optimization_barrier(filtered[0].astype(jnp.bfloat16))
    positions = jnp.arange(length, dtype=jnp.float32)

    def add_mode(total, mode_terms):
        residue, rate = mode_terms
        term = (residue * jnp.sqrt(2.0 * rate))[:, None] * jnp.exp(-rate[:, None] * positions[None, :])
        return (total + term, None)
    long_filter, unused = lax.scan(add_mode, jnp.zeros((streams.shape[1], length), jnp.float32), (residues, rates))
    gated_wide = gated.astype(jnp.float32)
    spectrum = jnp.fft.rfft(gated_wide, n=2 * length, axis=1) * jnp.fft.rfft(long_filter, n=2 * length, axis=1)
    conv = jnp.fft.irfft(spectrum, n=2 * length, axis=1)[:, :length].astype(jnp.float32)
    mixed = lax.optimization_barrier((conv + skip[:, None] * gated_wide).astype(jnp.bfloat16))
    return (query.astype(jnp.float32) * mixed.astype(jnp.float32)).astype(jnp.bfloat16)
```

```python
import jax
import jax.numpy as jnp
from jax import lax
from jax.experimental import pallas as pl
from jax.experimental.pallas import tpu as pltpu
from jax.sharding import PartitionSpec as P

F32 = jnp.float32
BF16 = jnp.bfloat16
WIDE = F32
SHORT = 3
MODES = 16
GROUP = 8
STEP = 16
LANES = 128
VMEM = 52 * 1024 * 1024
SMALL = 16 * 1024 * 1024


def cat(parts, axis=0):
    return jnp.concatenate(parts, axis=axis)


def iota(shape, dim):
    return lax.broadcasted_iota(jnp.int32, shape, dim)


def split(x):
    high = x.astype(BF16)
    return high, (x - high.astype(F32)).astype(BF16)


def filtered(load, rim, taps, count):
    lane = iota((16, LANES), 1)
    first, second = lane < 1, lane < 2
    before1, before2 = pltpu.roll(rim, 1, 1), pltpu.roll(rim, 2, 1)
    for k in range(count):
        here = load(k)
        turned1, turned2 = pltpu.roll(here, 1, 1), pltpu.roll(here, 2, 1)
        back1 = jnp.where(first, before1, turned1)
        back2 = jnp.where(second, before2, turned2)
        yield taps[0] * here.astype(F32) + taps[1] * back1.astype(F32) + taps[2] * back2.astype(F32)
        before1, before2 = turned1, turned2


def swap_blocks(tiles):
    lane = iota(tiles[0].shape, 1) // STEP
    tiles = [pltpu.roll(x, STEP * c, 1) if c else x for c, x in enumerate(tiles)]
    for d in (4, 2, 1):
        keep = (lane & d) == 0
        tiles = [jnp.where(keep, tiles[j], tiles[(j + d) % 8]) for j in range(8)]
    tiles = [tiles[-j % 8] for j in range(8)]
    return [pltpu.roll(x, LANES - STEP * j, 1) if j else x for j, x in enumerate(tiles)]


def spread(base):
    lane = iota(base.shape, 1) // STEP
    return cat([jnp.where(lane == c, base, jnp.zeros_like(base)) for c in range(GROUP)], 0)


def decay_in(rate):
    row = iota((STEP, LANES), 0).astype(F32)
    high, low = split(jnp.exp(rate * (row - float(STEP))))
    return cat([spread(high), spread(low)], 0)


def table_kernel(residues, rates, skips, tables):
    lane = iota((STEP, LANES), 1)
    place = (lane % STEP).astype(F32)
    row = iota((STEP, LANES), 0)
    after = (lane % STEP) >= row
    same = (lane % STEP) == row

    def tile(i, _):
        cols = pl.ds(pl.multiple_of(i * LANES, LANES), LANES)
        rate16, residue16 = rates[:, cols], residues[:, cols]
        weight16 = residue16 * jnp.sqrt(2.0 * rate16)
        skip16 = jnp.broadcast_to(skips[:, cols], (STEP, LANES))
        for j in range(LANES // GROUP):
            at = lane // STEP + GROUP * j
            rate = jnp.take_along_axis(rate16, at, axis=1)
            weight = jnp.take_along_axis(weight16, at, axis=1)
            skip = jnp.take_along_axis(skip16, at, axis=1)
            out = weight * jnp.exp(-rate * place)
            taps = jnp.broadcast_to(jnp.sum(out, axis=0, keepdims=True), (STEP, LANES))
            near = pltpu.roll(taps, 0, 1, stride=1, stride_axis=0)
            near = jnp.where(after, near, 0.0) + jnp.where(same, skip, 0.0)
            g = i * (LANES // GROUP) + j
            tables[g] = cat([*split(out), *split(near)], 0)
        return 0

    lax.fori_loop(0, rates.shape[1] // LANES, tile, 0)


def gate_kernel(streams, rims, taps, rates, gated, sums, state, xs, zs):
    tiles = streams.shape[2] // LANES
    pairs = streams.shape[1] // 16
    segment = streams.shape[2] // 8
    unroll = xs.shape[0]
    left = 7.0 - iota((8, LANES), 0).astype(F32)

    def step(i, _):
        for u in range(unroll):
            rows = pl.ds(pl.multiple_of((i * unroll + u) * 16, 16), 16)
            sides = []
            for s in (0, 1):
                tap = [
                    jnp.broadcast_to(taps[rows, pl.ds(3 * (s + 1) + j, 1)], (16, LANES)) for j in range(SHORT)
                ]
                load = lambda k, s=s, rows=rows: streams[s, rows, pl.ds(k * LANES, LANES)].astype(WIDE)
                sides.append(filtered(load, rims[s, rows, :].astype(WIDE), tap, tiles))
            for k, (a, b) in enumerate(zip(*sides)):
                xs[u, k % 2, pl.ds(k // 2 * 16, 16), :] = a * b
        for v in range(2 * unroll):
            g = i * 2 * unroll + v
            u, half = v // 2, v % 2
            lined = [
                cat([xs[u, odd, pl.ds(8 * half + c, 8, stride=16), :] for odd in (0, 1)], 0).astype(BF16)
                for c in range(GROUP)
            ]
            gated[g] = cat(swap_blocks(lined), 0)
        for v in range(2 * unroll):
            g = i * 2 * unroll + v
            x = gated[g]
            zs[v] = jnp.dot(cat([x, x], 1), decay_in(rates[pl.ds(g, 1), :]), preferred_element_type=F32)
        for v in range(2 * unroll):
            g = i * 2 * unroll + v
            rate = rates[pl.ds(g, 1), :]
            over = jnp.exp(-float(STEP) * rate)
            held = zs[v, 0:8, :]
            for k in range(1, 16):
                at = 16 * (k % 8) + 8 * (k // 8)
                held = held * over + zs[v, at : at + 8, :]
            sums[g] = held
            state[pl.ds(g, 1), :] = jnp.sum(
                held * jnp.exp(-float(segment) * rate * left), axis=0, keepdims=True
            )
        return 0

    lax.fori_loop(0, pairs // unroll, step, 0)


def query_kernel(streams, rims, taps, query):
    tiles = streams.shape[2] // LANES

    def pair(i, _):
        rows = pl.ds(pl.multiple_of(i * 16, 16), 16)
        tap = [jnp.broadcast_to(taps[rows, pl.ds(j, 1)], (16, LANES)) for j in range(SHORT)]
        load = lambda k: streams[0, rows, pl.ds(k * LANES, LANES)].astype(WIDE)
        for k, tile in enumerate(filtered(load, rims[0, rows, :].astype(WIDE), tap, tiles)):
            query[rows, pl.ds(k * LANES, LANES)] = tile.astype(BF16)
        return 0

    lax.fori_loop(0, streams.shape[1] // 16, pair, 0, unroll=2)


def mix_kernel(gated, sums, query, rates, tables, before, out, ys, zs):
    tiles = query.shape[1] // LANES
    pairs = query.shape[0] // 16
    segment = query.shape[1] // 8
    unroll = ys.shape[0]
    row = iota((8, LANES), 0)

    def step(i, _):
        for v in range(2 * unroll):
            g = i * 2 * unroll + v
            x = gated[g]
            zs[v] = jnp.dot(cat([x, x], 1), decay_in(rates[pl.ds(g, 1), :]), preferred_element_type=F32)
        for v in range(2 * unroll):
            g = i * 2 * unroll + v
            rate = rates[pl.ds(g, 1), :]
            over = jnp.exp(-float(STEP) * rate)
            first = jnp.broadcast_to(before[pl.ds(g, 1), :], (8, LANES))
            held = jnp.where(row == 0, first, pltpu.roll(sums[g], 1, 0))
            for d in (1, 2, 4):
                earlier = jnp.where(row < d, 0.0, pltpu.roll(held, d, 0))
                held = held + jnp.exp(-float(segment * d) * rate) * earlier
            for k in range(16):
                at = 16 * (k % 8) + 8 * (k // 8)
                entering = zs[v, at : at + 8, :]
                zs[v, at : at + 8, :] = held
                held = held * over + entering
        for v in range(2 * unroll):
            g = i * 2 * unroll + v
            x = gated[g]
            high, low = split(zs[v])
            base = tables[g]
            far_high, far_low, near_high, near_low = [spread(base[16 * n : 16 * n + 16]) for n in range(4)]
            zs[v] = jnp.dot(
                cat([high, high, low, x, x], 1),
                cat([far_high, far_low, far_high, near_high, near_low], 0),
                preferred_element_type=F32,
            )
        for v in range(2 * unroll):
            u, half = v // 2, v % 2
            lined = swap_blocks([zs[v, 16 * b : 16 * b + 16, :].astype(BF16) for b in range(8)])
            for c in range(GROUP):
                wide = lined[c].astype(F32)
                for odd in (0, 1):
                    ys[u, odd, pl.ds(8 * half + c, 8, stride=16), :] = wide[8 * odd : 8 * odd + 8]
        for u in range(unroll):
            rows = pl.ds(pl.multiple_of((i * unroll + u) * 16, 16), 16)
            for k in range(tiles):
                mixed = ys[u, k % 2, pl.ds(k // 2 * 16, 16), :].astype(BF16)
                cols = pl.ds(k * LANES, LANES)
                out[rows, cols] = query[rows, cols] * mixed
        return 0

    lax.fori_loop(0, pairs // unroll, step, 0)


def make_tables(residues, rates, skip):
    channels = rates.shape[1]
    groups = channels // GROUP
    return pl.pallas_call(
        table_kernel,
        out_shape=jax.ShapeDtypeStruct((groups, 4 * STEP, LANES), BF16),
        compiler_params=pltpu.CompilerParams(vmem_limit_bytes=SMALL),
        name="tables",
    )(residues, rates, skip[None, :])


def make_query(streams, rims, taps, block):
    channels, length = streams.shape[1:]
    return pl.pallas_call(
        query_kernel,
        grid=(channels // block,),
        in_specs=[
            pl.BlockSpec((1, block, length), lambda i: (0, i, 0)),
            pl.BlockSpec((1, block, LANES), lambda i: (0, i, 0)),
            pl.BlockSpec((block, 9), lambda i: (i, 0)),
        ],
        out_specs=pl.BlockSpec((block, length), lambda i: (i, 0)),
        out_shape=jax.ShapeDtypeStruct((channels, length), BF16),
        compiler_params=pltpu.CompilerParams(vmem_limit_bytes=VMEM),
        cost_estimate=pl.CostEstimate(flops=channels * length * 1024, bytes_accessed=4 * channels * length, transcendentals=0),
        name="query",
    )(streams, rims, taps)


def gate(streams, rims, taps, rates, block, unroll=8):
    channels, length = streams.shape[1:]
    groups = channels // GROUP
    rows = length // STEP
    bg = block // GROUP
    return pl.pallas_call(
        gate_kernel,
        grid=(channels // block,),
        in_specs=[
            pl.BlockSpec((pl.Element(2), pl.Element(block), pl.Element(length)), lambda i: (1, i * block, 0)),
            pl.BlockSpec((pl.Element(2), pl.Element(block), pl.Element(LANES)), lambda i: (1, i * block, 0)),
            pl.BlockSpec((block, 9), lambda i: (i, 0)),
            pl.BlockSpec((bg, LANES), lambda i: (i, 0)),
        ],
        out_specs=[
            pl.BlockSpec((bg, rows, LANES), lambda i: (i, 0, 0)),
            pl.BlockSpec((bg, 8, LANES), lambda i: (i, 0, 0)),
            pl.BlockSpec((bg, LANES), lambda i: (i, 0)),
        ],
        out_shape=[
            jax.ShapeDtypeStruct((groups, rows, LANES), BF16),
            jax.ShapeDtypeStruct((groups, 8, LANES), F32),
            jax.ShapeDtypeStruct((groups, LANES), F32),
        ],
        scratch_shapes=[pltpu.VMEM((unroll, 2, rows, LANES), F32), pltpu.VMEM((2 * unroll, rows, LANES), F32)],
        compiler_params=pltpu.CompilerParams(vmem_limit_bytes=VMEM),
        name="gate",
    )(streams, rims, taps, rates)


def mix(gated, sums, query, rates, tables, before, block, unroll=8):
    channels, length = query.shape
    rows = length // STEP
    bg = block // GROUP
    return pl.pallas_call(
        mix_kernel,
        grid=(channels // block,),
        in_specs=[
            pl.BlockSpec((bg, rows, LANES), lambda i: (i, 0, 0)),
            pl.BlockSpec((bg, 8, LANES), lambda i: (i, 0, 0)),
            pl.BlockSpec((block, length), lambda i: (i, 0)),
            pl.BlockSpec((bg, LANES), lambda i: (i, 0)),
            pl.BlockSpec((bg, 4 * STEP, LANES), lambda i: (i, 0, 0)),
            pl.BlockSpec((bg, LANES), lambda i: (i, 0)),
        ],
        out_specs=pl.BlockSpec((block, length), lambda i: (i, 0)),
        out_shape=jax.ShapeDtypeStruct((channels, length), BF16),
        scratch_shapes=[pltpu.VMEM((unroll, 2, rows, LANES), F32), pltpu.VMEM((2 * unroll, rows, LANES), F32)],
        compiler_params=pltpu.CompilerParams(vmem_limit_bytes=VMEM),
        name="mix",
    )(gated, sums, query, rates, tables, before)


def states_before(state, rates, length):
    axis = "ctx"
    index = lax.axis_index(axis)
    devices = lax.axis_size(axis)

    def decay(times):
        return jnp.exp(-float(length) * rates * jnp.asarray(times, F32))

    before = jnp.zeros_like(state)
    total = state
    span = 1
    for size in (2, 4, 4):
        place = (index // span) % size

        def moved(by):
            pairs = []
            for i in range(devices):
                at = (i // span) % size
                pairs.append((i, i + ((at + by) % size - at) * span))
            return lax.ppermute(total, axis, pairs)

        others = [moved(by) for by in range(1, size)]
        prefix = jnp.zeros_like(state)
        whole = decay(span * (size - 1 - place)) * total
        for by, other in enumerate(others, 1):
            at = (place - by) % size
            valid = by <= place
            prefix = prefix + jnp.where(valid, decay(span * jnp.where(valid, by - 1, 0)) * other, 0.0)
            whole = whole + decay(span * (size - 1 - at)) * other
        before = before + decay(index % span) * prefix
        total = whole
        span *= size
    return before


def on_device(streams, short_filters, residues, rates, skip):
    channels, length = streams.shape[1:]
    groups = channels // GROUP

    def by_group(x):
        return x.T.reshape(groups, GROUP * MODES)

    devices = lax.axis_size("ctx")
    edge = streams[:, :, length - (SHORT - 1) :]
    rims = lax.ppermute(edge, "ctx", [(i, i + 1) for i in range(devices - 1)])
    rims = jnp.pad(rims, ((0, 0), (0, 0), (LANES - (SHORT - 1), 0)))
    taps = short_filters.reshape(9, channels).T
    rate = by_group(rates)
    tables = make_tables(residues, rates, skip)
    gated, sums, state = gate(streams, rims, taps, rate, 128)
    query = make_query(streams, rims, taps, 128)
    before = states_before(state, rate, length)
    return mix(gated, sums, query, rate, tables, before, 128)


def solution(mesh):
    in_specs = (P(None, "tp", "ctx"), P(None, None, "tp"), P(None, "tp"), P(None, "tp"), P("tp"))
    out_specs = P("tp", "ctx")
    return jax.shard_map(
        on_device, mesh=mesh, in_specs=in_specs, out_specs=out_specs, check_vma=False
    )
```

```python
import jax
import jax.numpy as jnp
from jax import lax
from jax.experimental import pallas as pl
from jax.experimental.pallas import tpu as pltpu
from jax.sharding import PartitionSpec as P

F32 = jnp.float32
BF16 = jnp.bfloat16
BATCH = 2
WIDE = 8
SHORT = 3
MODES = 16
GROUP = 8
STEP = 16
LANES = 128
MIB = 1024 * 1024


def cat(parts, axis=0):
    return jnp.concatenate(parts, axis=axis)


def iota(shape, dim):
    return lax.broadcasted_iota(jnp.int32, shape, dim)


def split(x):
    high = x.astype(BF16)
    return high, (x - high.astype(F32)).astype(BF16)


def filtered(load, rim, taps, count):
    lane = iota((16, LANES), 1)
    first, second = lane < 1, lane < 2
    before1, before2 = pltpu.roll(rim, 1, 1), pltpu.roll(rim, 2, 1)
    for k in range(count):
        here = load(k)
        turned1, turned2 = pltpu.roll(here, 1, 1), pltpu.roll(here, 2, 1)
        back1 = jnp.where(first, before1, turned1)
        back2 = jnp.where(second, before2, turned2)
        yield taps[0] * here.astype(F32) + taps[1] * back1.astype(F32) + taps[2] * back2.astype(F32)
        before1, before2 = turned1, turned2


def swap_blocks(tiles):
    lane = iota(tiles[0].shape, 1) // STEP
    tiles = [pltpu.roll(x, STEP * c, 1) if c else x for c, x in enumerate(tiles)]
    for d in (4, 2, 1):
        keep = (lane & d) == 0
        tiles = [jnp.where(keep, tiles[j], tiles[(j + d) % 8]) for j in range(8)]
    tiles = [tiles[-j % 8] for j in range(8)]
    return [pltpu.roll(x, LANES - STEP * j, 1) if j else x for j, x in enumerate(tiles)]


def spread(base):
    lane = iota(base.shape, 1) // STEP
    return cat([jnp.where(lane == c, base, jnp.zeros_like(base)) for c in range(GROUP)], 0)


def decay_in(rate):
    row = iota((STEP, LANES), 0).astype(F32)
    high, low = split(jnp.exp(rate * (row - float(STEP))))
    return cat([spread(high), spread(low)], 0)


def table_kernel(residues, rates, skips, tables):
    lane = iota((STEP, LANES), 1)
    place = (lane % STEP).astype(F32)
    row = iota((STEP, LANES), 0)
    after = (lane % STEP) >= row
    same = (lane % STEP) == row

    def tile(i, _):
        cols = pl.ds(pl.multiple_of(i * LANES, LANES), LANES)
        rate16, residue16 = rates[:, cols], residues[:, cols]
        weight16 = residue16 * jnp.sqrt(2.0 * rate16)
        skip16 = jnp.broadcast_to(skips[:, cols], (STEP, LANES))
        for j in range(LANES // GROUP):
            at = lane // STEP + GROUP * j
            rate = jnp.take_along_axis(rate16, at, axis=1)
            weight = jnp.take_along_axis(weight16, at, axis=1)
            skip = jnp.take_along_axis(skip16, at, axis=1)
            out = weight * jnp.exp(-rate * place)
            taps = jnp.broadcast_to(jnp.sum(out, axis=0, keepdims=True), (STEP, LANES))
            near = pltpu.roll(taps, 0, 1, stride=1, stride_axis=0)
            near = jnp.where(after, near, 0.0) + jnp.where(same, skip, 0.0)
            g = i * (LANES // GROUP) + j
            tables[g] = cat([*split(out), *split(near)], 0)
        return 0

    lax.fori_loop(0, rates.shape[1] // LANES, tile, 0)


def moves(source, target, semaphores, rows, dim=0):
    def copy(i):
        block = (slice(None),) * dim + (pl.ds(pl.multiple_of(i * rows, rows), rows),)
        return pltpu.make_async_copy(source.at[block], target.at[block], semaphores.at[i])

    return copy


def step_decay(rates, at, count, times):
    return jnp.exp(-float(times) * rates[pl.ds(at, count), :])[:, None, :]


def gate_kernel(source, rims, taps, rates, gated_out, sums_out, state, streams, gated, sums, xs, zs, arrived, sent, sent_sums):
    tiles = streams.shape[2] // LANES
    pairs = streams.shape[1] // 16
    segment = streams.shape[2] // 8
    unroll = zs.shape[0] // 2
    steps = pairs // unroll
    fetch = moves(source.at[pl.ds(1, 2)], streams, arrived, 16 * unroll, 1)
    send = moves(gated, gated_out, sent, 2 * unroll)
    send_sums = moves(sums, sums_out, sent_sums, 2 * unroll)
    for i in range(steps):
        fetch(i).start()
    left = 7.0 - iota((1, 8, LANES), 1).astype(F32)

    def step(i, _):
        fetch(i).wait()
        first = pl.multiple_of(i * 2 * unroll, 2 * unroll)
        for u in range(unroll):
            rows = pl.ds(pl.multiple_of((i * unroll + u) * 16, 16), 16)
            sides = []
            for s in (0, 1):
                tap = [
                    jnp.broadcast_to(taps[rows, pl.ds(3 * (s + 1) + j, 1)], (16, LANES)) for j in range(SHORT)
                ]
                load = lambda k, s=s, rows=rows: streams[s, rows, pl.ds(k * LANES, LANES)].astype(F32)
                sides.append(filtered(load, rims[s + 1, rows, :].astype(F32), tap, tiles))
            for k, (a, b) in enumerate(zip(*sides)):
                xs[pl.ds((u * 2 + k % 2) * LANES + k // 2 * 16, 16), :] = a * b
        for u in range(0, unroll, BATCH):
            for half in (0, 1):
                lined = swap_blocks(
                    [xs[pl.ds(u * 256 + 8 * half + c, 16 * BATCH, stride=16), :] for c in range(GROUP)]
                )
                for w in range(BATCH):
                    gated[first + 2 * (u + w) + half] = cat(
                        [tile[16 * w : 16 * w + 16] for tile in lined], 0
                    ).astype(BF16)
        for v in range(2 * unroll):
            x = gated[first + v]
            zs[v] = jnp.dot(
                cat([x, x], 1), decay_in(rates[pl.ds(first + v, 1), :]), preferred_element_type=F32
            )
        for v in range(0, 2 * unroll, WIDE):
            some = pl.ds(first + v, WIDE)
            over = jnp.broadcast_to(step_decay(rates, first + v, WIDE, STEP), (WIDE, 8, LANES))
            held = zs[v : v + WIDE, 0:8, :]
            for k in range(1, 16):
                at = 16 * (k % 8) + 8 * (k // 8)
                held = held * over + zs[v : v + WIDE, at : at + 8, :]
            sums[some] = held
            rate = rates[some, :][:, None, :]
            state[some, :] = jnp.sum(held * jnp.exp(-float(segment) * rate * left), axis=1)
        send(i).start()
        send_sums(i).start()
        return 0

    lax.fori_loop(0, steps, step, 0)
    for i in range(steps):
        send(i).wait()
        send_sums(i).wait()


def query_kernel(source, rims, taps, query_out, streams, query, arrived, sent):
    tiles = streams.shape[2] // LANES
    unroll = 4
    steps = streams.shape[1] // 16 // unroll
    fetch = moves(source.at[pl.ds(0, 1)], streams, arrived, 16 * unroll, 1)
    send = moves(query, query_out, sent, 16 * unroll)
    for i in range(steps):
        fetch(i).start()

    def step(i, _):
        fetch(i).wait()
        for u in range(unroll):
            rows = pl.ds(pl.multiple_of((i * unroll + u) * 16, 16), 16)
            tap = [jnp.broadcast_to(taps[rows, pl.ds(j, 1)], (16, LANES)) for j in range(SHORT)]
            load = lambda k, rows=rows: streams[0, rows, pl.ds(k * LANES, LANES)].astype(F32)
            for k, tile in enumerate(filtered(load, rims[0, rows, :].astype(F32), tap, tiles)):
                query[rows, pl.ds(k * LANES, LANES)] = tile.astype(BF16)
        send(i).start()
        return 0

    lax.fori_loop(0, steps, step, 0)
    for i in range(steps):
        send(i).wait()


def mix_kernel(gated_in, sums_in, query_in, rates, tables_in, before, target, gated, sums, query, tables, out, ys, zs, arrived, sent):
    tiles = query.shape[1] // LANES
    pairs = query.shape[0] // 16
    segment = query.shape[1] // 8
    unroll = zs.shape[1]
    row = iota((WIDE, 8, LANES), 1)

    steps = pairs // unroll
    inputs = (
        moves(gated_in, gated, arrived.at[0], 2 * unroll),
        moves(sums_in, sums, arrived.at[1], 2 * unroll),
        moves(tables_in, tables, arrived.at[2], 2 * unroll),
        moves(query_in, query, arrived.at[3], 16 * unroll),
    )
    send = moves(out, target, sent, 16 * unroll)
    for i in range(steps):
        for copy in inputs:
            copy(i).start()

    def step(i, _):
        for copy in inputs:
            copy(i).wait()
        base_group = pl.multiple_of(i * 2 * unroll, 2 * unroll)
        for v in range(2 * unroll):
            x = gated[base_group + v]
            zs[v % 2, v // 2] = jnp.dot(
                cat([x, x], 1), decay_in(rates[pl.ds(base_group + v, 1), :]), preferred_element_type=F32
            )
        for v in range(0, 2 * unroll, WIDE):
            some = pl.ds(base_group + v, WIDE)
            over = jnp.broadcast_to(step_decay(rates, base_group + v, WIDE, STEP), (WIDE, 8, LANES))
            entry = jnp.broadcast_to(before[some, :][:, None, :], (WIDE, 8, LANES))
            held = jnp.where(row == 0, entry, pltpu.roll(sums[some], 1, 1))
            for d in (1, 2, 4):
                earlier = jnp.where(row < d, 0.0, pltpu.roll(held, d, 1))
                held = held + step_decay(rates, base_group + v, WIDE, segment * d) * earlier
            held = [held[w] for w in range(WIDE)]
            for k in range(16):
                at = 16 * (k % 8) + 8 * (k // 8)
                for w in range(WIDE):
                    z = zs.at[(v + w) % 2, (v + w) // 2, pl.ds(at, 8)]
                    entering = z[...]
                    z[...] = held[w]
                    held[w] = held[w] * over[w] + entering
        for v in range(2 * unroll):
            x = gated[base_group + v]
            high, low = split(zs[v % 2, v // 2])
            base = tables[base_group + v]
            far_high, far_low, near_high, near_low = [spread(base[16 * n : 16 * n + 16]) for n in range(4)]
            zs[v % 2, v // 2] = jnp.dot(
                cat([high, high, low, x, x], 1),
                cat([far_high, far_low, far_high, near_high, near_low], 0),
                preferred_element_type=F32,
            )
        for u in range(0, unroll, 2 * BATCH):
            for half in (0, 1):
                for odd in (0, 1):
                    lined = swap_blocks(
                        [
                            zs[half, u : u + 2 * BATCH, 16 * b + 8 * odd : 16 * b + 8 * odd + 8, :].reshape(16 * BATCH, LANES)
                            for b in range(8)
                        ]
                    )
                    for c in range(GROUP):
                        ys[pl.ds((odd * unroll + u) * LANES + 8 * half + c, 16 * BATCH, stride=16), :] = lined[c]
        for u in range(unroll):
            rows = pl.ds(pl.multiple_of((i * unroll + u) * 16, 16), 16)
            for k in range(tiles):
                mixed = ys[pl.ds((k % 2 * unroll + u) * LANES + k // 2 * 16, 16), :].astype(BF16)
                cols = pl.ds(k * LANES, LANES)
                out[rows, cols] = query[rows, cols] * mixed
        send(i).start()
        return 0

    lax.fori_loop(0, steps, step, 0)
    for i in range(steps):
        send(i).wait()


def make_tables(residues, rates, skip):
    channels = rates.shape[1]
    groups = channels // GROUP
    return pl.pallas_call(
        table_kernel,
        out_shape=jax.ShapeDtypeStruct((groups, 4 * STEP, LANES), BF16),
        compiler_params=pltpu.CompilerParams(vmem_limit_bytes=8 * MIB),
        name="tables",
    )(residues, rates, skip[None, :])


WHOLE = pl.BlockSpec(memory_space=pltpu.VMEM)
APART = pl.BlockSpec(memory_space=pltpu.HBM)


def make_query(streams, rims, taps):
    channels, length = streams.shape[1:]
    return pl.pallas_call(
        query_kernel,
        in_specs=[APART, WHOLE, WHOLE],
        out_specs=APART,
        out_shape=jax.ShapeDtypeStruct((channels, length), BF16),
        scratch_shapes=[
            pltpu.VMEM((1, channels, length), BF16),
            pltpu.VMEM((channels, length), BF16),
            pltpu.SemaphoreType.DMA((channels // 64,)),
            pltpu.SemaphoreType.DMA((channels // 64,)),
        ],
        compiler_params=pltpu.CompilerParams(vmem_limit_bytes=50 * MIB),
        name="query",
    )(streams, rims, taps)


def gate(streams, rims, taps, rates, unroll=8):
    channels, length = streams.shape[1:]
    groups = channels // GROUP
    rows = length // STEP
    return pl.pallas_call(
        gate_kernel,
        in_specs=[APART, WHOLE, WHOLE, WHOLE],
        out_specs=[APART, APART, WHOLE],
        out_shape=[
            jax.ShapeDtypeStruct((groups, rows, LANES), BF16),
            jax.ShapeDtypeStruct((groups, 8, LANES), F32),
            jax.ShapeDtypeStruct((groups, LANES), F32),
        ],
        scratch_shapes=[
            pltpu.VMEM((2, channels, length), BF16),
            pltpu.VMEM((groups, rows, LANES), BF16),
            pltpu.VMEM((groups, 8, LANES), F32),
            pltpu.VMEM((unroll * 2 * rows, LANES), F32),
            pltpu.VMEM((2 * unroll, rows, LANES), F32),
            pltpu.SemaphoreType.DMA((channels // (16 * unroll),)),
            pltpu.SemaphoreType.DMA((channels // (16 * unroll),)),
            pltpu.SemaphoreType.DMA((channels // (16 * unroll),)),
        ],
        compiler_params=pltpu.CompilerParams(vmem_limit_bytes=50 * MIB),
        name="gate",
    )(streams, rims, taps, rates)


def mix(gated, sums, query, rates, tables, before, unroll=16):
    channels, length = query.shape
    rows = length // STEP
    return pl.pallas_call(
        mix_kernel,
        in_specs=[APART, APART, APART, WHOLE, APART, WHOLE],
        out_specs=APART,
        out_shape=jax.ShapeDtypeStruct((channels, length), BF16),
        scratch_shapes=[
            pltpu.VMEM(gated.shape, BF16),
            pltpu.VMEM(sums.shape, F32),
            pltpu.VMEM((channels, length), BF16),
            pltpu.VMEM(tables.shape, BF16),
            pltpu.VMEM((channels, length), BF16),
            pltpu.VMEM((unroll * 2 * rows, LANES), F32),
            pltpu.VMEM((2, unroll, rows, LANES), F32),
            pltpu.SemaphoreType.DMA((4, channels // (16 * unroll))),
            pltpu.SemaphoreType.DMA((channels // (16 * unroll),)),
        ],
        compiler_params=pltpu.CompilerParams(vmem_limit_bytes=50 * MIB),
        name="mix",
    )(gated, sums, query, rates, tables, before)


def states_before(state, rates, length, beside):
    axis = "ctx"
    index = lax.axis_index(axis)
    devices = lax.axis_size(axis)

    def decay(times):
        return jnp.exp(-float(length) * rates * jnp.asarray(times, F32))

    before = jnp.zeros_like(state)
    total = state
    span = 1
    made = []
    for size, work in zip((2, 4, 4), beside):
        place = (index // span) % size

        def moved(by):
            pairs = []
            for i in range(devices):
                at = (i // span) % size
                pairs.append((i, i + ((at + by) % size - at) * span))
            return lax.ppermute(total, axis, pairs)

        others = [moved(by) for by in range(1, size)]
        prefix = jnp.zeros_like(state)
        whole = decay(span * (size - 1 - place)) * total
        for by, other in enumerate(others, 1):
            at = (place - by) % size
            valid = by <= place
            prefix = prefix + jnp.where(valid, decay(span * jnp.where(valid, by - 1, 0)) * other, 0.0)
            whole = whole + decay(span * (size - 1 - at)) * other
        before = before + decay(index % span) * prefix
        total = whole
        if work is not None:
            total, work = lax.optimization_barrier((total, work))
            made.append(work)
        span *= size
    return before, made


def on_device(streams, short_filters, residues, rates, skip):
    channels, length = streams.shape[1:]
    groups = channels // GROUP

    def by_group(x):
        return x.T.reshape(groups, GROUP * MODES)

    devices = lax.axis_size("ctx")
    edge = streams[:, :, length - (SHORT - 1) :]
    rims = lax.ppermute(edge, "ctx", [(i, i + 1) for i in range(devices - 1)])
    rims = jnp.pad(rims, ((0, 0), (0, 0), (LANES - (SHORT - 1), 0)))
    taps = short_filters.reshape(9, channels).T
    rate = by_group(rates)
    gated, sums, state = gate(streams, rims, taps, rate)
    tables = make_tables(residues, rates, skip)
    query = make_query(streams, rims, taps)
    before, (query,) = states_before(state, rate, length, (None, query, None))
    return mix(gated, sums, query, rate, tables, before)


def solution(mesh):
    in_specs = (P(None, "tp", "ctx"), P(None, None, "tp"), P(None, "tp"), P(None, "tp"), P("tp"))
    out_specs = P("tp", "ctx")
    return jax.shard_map(
        on_device, mesh=mesh, in_specs=in_specs, out_specs=out_specs, check_vma=False
    )
```
